32 devices in a mesh: head: 4 (over y, x), seq: 8 (over z, core).
Axes of the slice: x: 2, y: 2, z: 4, core: 2. Of those that a mesh axis runs over, the one named last changes fastest.
Arguments:
- q_nope: bfloat16 [1024, 16384], P('seq', 'head'), may hold values from -6 to 6
- q_rope: bfloat16 [1024, 8192], P('seq', 'head'), may hold values from -128 to 128
- kv_latent: bfloat16 [1024, 576], P('seq'), may hold values from -10 to 10
- group_ids: int32 [1024], replicated, may hold values from 0 to 15, never falling along the last dimension, each value on 1 to 128 neighbouring positions
- w_uk: bfloat16 [128, 128, 512], P('head'), may hold values from -0.5 to 0.5
- w_uv: bfloat16 [128, 512, 128], P('head'), may hold values from -0.25 to 0.25
- moe_in: bfloat16 [2048, 7168], P('seq', 'head'), may hold values from -6 to 6
- expert_ids: int32 [2048, 2], P('seq'), may hold values from 0 to 7, all different within a row; in each aligned block of 256 rows (0 to 255, 256 to 511, ...) at most 128 rows name the same one
- gate_w: float32 [2048, 2], P('seq'), may hold values from 0.1 to 1
- w_gate: bfloat16 [8, 7168, 1024], P('seq', 'head'), may hold values from -0.0625 to 0.0625
- w_up: bfloat16 [8, 7168, 1024], P('seq', 'head'), may hold values from -0.0625 to 0.0625
- w_down: bfloat16 [8, 1024, 7168], P('seq', None, 'head'), may hold values from -0.1875 to 0.1875
Outputs:
- attn_out: bfloat16 [1024, 16384], P('seq', 'head')
- moe_out: bfloat16 [2048, 7168], P('seq', 'head')
The draws below stay inside these ranges and needn't reach their ends.
Inputs may be any that keep to these rules, and one draw needn't show every extreme that they name: `expert_ids`: each row names 2 different experts. Among the routes of one aligned block of 256 rows (the rows of one index of seq) no expert is named more than 128 times, a bound that some block reaches. `group_ids`: never falls along the rows; each group holds 1 to 128 consecutive tokens, one exactly 128.
All inputs are finite; a program needn't handle non-finite values.
Results may differ from the reference program's by a relative error of at most 0.007.
Values may be sent and summed in bfloat16 or wider, within the bound.
A program may use at most 192 MiB of HBM per device.

```python
import math
import jax
import jax.numpy as jnp
import numpy as np
from jax import lax

D = 7168
HEADS = 128
NOPE = 128
ROPE = 64
LAT = 512
VDIM = 128
FF = 1024
TOPW = 2
ATT_TOK = 128
MOE_TOK = 256
EXPERTS = 8
CAP = 128
ATT_ROWS = 1024
MOE_ROWS = 2048
GROUPS = 16
N_SEQ = 8


def draw_kv_latent(key, part):
    latent = jnp.clip(jax.random.normal(jax.random.fold_in(key, 11), (ATT_ROWS, LAT), jnp.float32), -6.0, 6.0)
    rotary = jnp.clip(jax.random.normal(jax.random.fold_in(key, 13), (ATT_ROWS, ROPE), jnp.float32), -6.0, 6.0)
    return jnp.concatenate([latent, rotary], axis=1).astype(jnp.bfloat16)


def draw_q_rope(key, part):
    noise = jax.random.normal(jax.random.fold_in(key, 17), (ATT_ROWS // 8, 8, HEADS, ROPE), jnp.float32)
    noise = jnp.clip(noise, -6.0, 6.0)
    values = noise
    return values.reshape(ATT_ROWS, HEADS * ROPE).astype(jnp.bfloat16)


def shard_levels(key, shape, split, least, high):
    loudness = 1.0
    for axis_at, parts in split:
        heights = jax.random.uniform(jax.random.fold_in(jax.random.fold_in(key, 6), axis_at), (parts,), jnp.float32, least / len(split), high / len(split))
        loudness = loudness * jnp.repeat(jnp.exp(heights), shape[axis_at] // parts).reshape((-1,) + (1,) * (len(shape) - 1 - axis_at))
    return loudness


def split_up(number_of, total, reach, slope):
    weights = [(1 << 20) // math.isqrt(grade ** slope) + 1 for grade in range(2, number_of + 1)]
    spare, given = total - reach - (number_of - 1), [1] * (number_of - 1)
    while spare > 0:
        movable = [i for i in range(number_of - 1) if given[i] < reach]
        mass, budget = sum([weights[i] for i in movable]), spare
        for i in movable:
            more = min(reach - given[i], max(1, budget * weights[i] // mass), spare)
            given[i] = given[i] + more
            spare = spare - more
    return np.array([reach] + given)


def ragged_sizes(stream_key, number_of, total, most, slope):
    if number_of == 2:
        one = jax.random.randint(stream_key, (), max(1, total - most), min(most, total - 1) + 1)
        return jnp.stack([one, total - one])
    tallies = jnp.asarray(split_up(number_of, total, most, slope), jnp.int32)
    twos = (number_of - 1) // 2
    source_of, sink = tallies[1:1 + 2 * twos:2], tallies[2:2 + 2 * twos:2]
    room = jnp.minimum(source_of - 1, most - sink)
    shifted = jax.random.randint(jax.random.fold_in(stream_key, 1), (twos,), 0, 1 << 20) % (room + 1)
    tallies = tallies.at[1:1 + 2 * twos:2].set(source_of - shifted).at[2:2 + 2 * twos:2].set(sink + shifted)
    return tallies[jax.random.permutation(jax.random.fold_in(stream_key, 2), number_of)]


def assign_block(own_key, own, number, rows, count, top, most, lean):
    order = jax.random.permutation(own_key, count)
    crowded, usual = load_shares(count, rows * top, most, lean, True), load_shares(count, rows * top, most, lean, False)
    places = jnp.arange(count)

    def named(lengths, rotation):
        used = int((lengths > 0).sum())
        fixed = max(1, used // 4)
        shifted = fixed + (places - fixed + rotation * (used - fixed)) % max(1, count - fixed)
        return jnp.zeros((count,), jnp.int32).at[order[jnp.where(places < fixed, places, shifted)]].set(jnp.asarray(lengths, jnp.int32))

    lengths = jnp.where(number % 4 == 0, named(crowded, number // 4), named(usual, number - number // 4 - 1))
    mixed = jax.random.permutation(jax.random.fold_in(own, 3), count)
    giver, taker = mixed[0:count // 2 * 2:2], mixed[1:count // 2 * 2:2]
    slack = jnp.minimum(lengths[giver] - 1, most - lengths[taker]) // 2
    slack = jnp.where((giver == order[0]) | (taker == order[0]) | (lengths[taker] == 0), 0, jnp.maximum(slack, 0))
    shifted = jax.random.randint(jax.random.fold_in(own, 4), (count // 2,), 0, 1 << 20) % (slack + 1)
    lengths = lengths.at[giver].add(-shifted).at[taker].add(shifted)
    labels = jnp.searchsorted(jnp.cumsum(lengths), jnp.arange(rows * top), side="right").astype(jnp.int32)
    grid = labels.reshape(top, rows).T
    grid = grid[jax.random.permutation(jax.random.fold_in(own, 1), rows)]
    rotation = jax.random.randint(jax.random.fold_in(own, 2), (rows, 1), 0, top)
    return jnp.take_along_axis(grid, (jnp.arange(top)[None, :] + rotation) % top, axis=1)


def load_shares(amount, total, limit, lean, full):
    portions = [(1 << 20) // math.isqrt(standing ** lean) + 1 for standing in range(1, amount + 1)]
    largest = limit if full else min(limit, max(-(-total // amount), total * portions[0] // sum(portions)))
    least = 1 if total - largest >= amount - 1 else 0
    holding, spare = [largest] + [least] * (amount - 1), total - largest - least * (amount - 1)
    while spare > 0:
        movable = [i for i in range(1, amount) if holding[i] < largest] or [i for i in range(1, amount) if holding[i] < limit]
        whole, remaining = sum([portions[i] for i in movable]), spare
        for i in movable:
            more = min(limit - holding[i], max(1, remaining * portions[i] // whole), spare)
            holding[i] = holding[i] + more
            spare = spare - more
    return np.array(holding)


def bell_draw(rng, extent, deviation, limit, split=(), kind=jnp.bfloat16):
    drawn = jax.random.normal(rng, extent, jnp.float32) * deviation
    if len(split) > 0:
        drawn = shard_levels(rng, extent, split, -0.22, 0.18) * drawn
    return jnp.clip(drawn, min=-limit, max=limit).astype(kind)


def setup_inputs(seed: int = 0) -> dict:
    streams_of = jax.random.split(jax.random.key(seed), 13)
    q_nope = bell_draw(streams_of[0], (ATT_ROWS, HEADS * NOPE), 1.0, 6.0, ((0, 8), (1, 4)))
    q_rope = draw_q_rope(jax.random.fold_in(streams_of[12], 71), 0)
    kv_latent = draw_kv_latent(jax.random.fold_in(streams_of[12], 71), 0)
    group_ids = jnp.searchsorted(jnp.cumsum(ragged_sizes(streams_of[3], GROUPS, ATT_ROWS, ATT_TOK, 1)), jnp.arange(ATT_ROWS), side="right").astype(jnp.int32)
    w_uk = bell_draw(streams_of[4], (HEADS, NOPE, LAT), NOPE ** -0.5, 0.5, ((0, 4),))
    w_uv = bell_draw(streams_of[5], (HEADS, LAT, VDIM), LAT ** -0.5, 0.25, ((0, 4),))
    moe_in = bell_draw(streams_of[6], (MOE_ROWS, D), 1.0, 6.0, ((0, 8), (1, 4)))
    expert_ids_keys = jax.random.split(jax.random.fold_in(streams_of[7], 1), MOE_ROWS // MOE_TOK)
    expert_ids_turns = jax.random.permutation(jax.random.fold_in(streams_of[7], 3), MOE_ROWS // MOE_TOK)
    expert_ids = jax.vmap(lambda own, number: assign_block(jax.random.fold_in(streams_of[7], 2), own, number, MOE_TOK, EXPERTS, TOPW, CAP, 2))(expert_ids_keys, expert_ids_turns).reshape((MOE_ROWS, TOPW))
    gate_w = jnp.clip(jnp.exp(math.log(1.0) - 2.3025851 * jax.random.uniform(streams_of[8], (MOE_ROWS, TOPW), jnp.float32) ** shard_levels(streams_of[8], (MOE_ROWS, TOPW), ((0, 8),), -0.2, 0.2)), 0.1, 1.0)
    w_gate = bell_draw(streams_of[9], (EXPERTS, D, FF), D ** -0.5, 0.0625, ((0, 8), (1, 4)))
    w_up = bell_draw(streams_of[10], (EXPERTS, D, FF), D ** -0.5, 0.0625, ((0, 8), (1, 4)))
    w_down = bell_draw(streams_of[11], (EXPERTS, FF, D), FF ** -0.5, 0.1875, ((0, 8), (2, 4)))
    return dict(q_nope=q_nope, q_rope=q_rope, kv_latent=kv_latent, group_ids=group_ids, w_uk=w_uk, w_uv=w_uv, moe_in=moe_in, expert_ids=expert_ids, gate_w=gate_w, w_gate=w_gate, w_up=w_up, w_down=w_down)


def attend_block(query_nope, query_rope, key_block, key_ids, query_ids, w_uk, w_uv):
    tok_count = query_nope.shape[0]
    head_count = w_uk.shape[0]
    nope_width = w_uk.shape[1]
    lat_width = w_uk.shape[2]
    rope_width = query_rope.shape[1] // head_count
    q_split = query_nope.reshape(tok_count, head_count, nope_width).astype(jnp.float32)
    r_split = query_rope.reshape(tok_count, head_count, rope_width).astype(jnp.float32)
    q_latent = jnp.einsum("thn,hnl->htl", q_split, w_uk.astype(jnp.float32)).astype(jnp.bfloat16)
    q_latent = lax.optimization_barrier(q_latent)
    latent = key_block[:, :lat_width].astype(jnp.float32)
    rotary = key_block[:, lat_width:].astype(jnp.float32)
    scale_factor = (nope_width + rope_width) ** -0.5
    scores = jnp.einsum("htl,kl->htk", q_latent.astype(jnp.float32), latent)
    scores = (scores + jnp.einsum("thr,kr->htk", r_split, rotary)) * scale_factor
    key_count = key_block.shape[0]
    query_pos = jnp.arange(tok_count, dtype=jnp.int32) + (key_count - tok_count)
    key_pos = jnp.arange(key_count, dtype=jnp.int32)
    allowed = (key_ids[None, :] == query_ids[:, None]) & (key_pos[None, :] <= query_pos[:, None])
    scores = jnp.where(allowed[None], scores, -jnp.inf)
    highest = jnp.max(scores, axis=2, keepdims=True)
    expo = jnp.exp(scores - highest)
    probs = (expo / jnp.sum(expo, axis=2, keepdims=True)).astype(jnp.bfloat16)
    probs = lax.optimization_barrier(probs)
    mixed_latent = jnp.einsum("htk,kl->htl", probs.astype(jnp.float32), latent).astype(jnp.bfloat16)
    mixed_latent = lax.optimization_barrier(mixed_latent)
    heads_out = jnp.einsum("htl,hlv->thv", mixed_latent.astype(jnp.float32), w_uv.astype(jnp.float32))
    return heads_out.astype(jnp.bfloat16).reshape(tok_count, head_count * w_uv.shape[2])


def reference(q_nope, q_rope, kv_latent, group_ids, w_uk, w_uv, moe_in, expert_ids, gate_w, w_gate, w_up, w_down):
    padded_kv = jnp.concatenate([jnp.zeros((ATT_TOK, LAT + ROPE), jnp.bfloat16), kv_latent], axis=0)
    padded_ids = jnp.concatenate([jnp.full((ATT_TOK,), -1, jnp.int32), group_ids.astype(jnp.int32)])
    query_blocks = q_nope.reshape(N_SEQ, ATT_TOK, HEADS * NOPE)
    rope_blocks = q_rope.reshape(N_SEQ, ATT_TOK, HEADS * ROPE)

    def one_block(inputs):
        block_idx, query_nope, query_rope = inputs
        start = (block_idx * ATT_TOK).astype(jnp.int32)
        key_block = lax.dynamic_slice_in_dim(padded_kv, start, 2 * ATT_TOK, 0)
        key_ids = lax.dynamic_slice_in_dim(padded_ids, start, 2 * ATT_TOK, 0)
        query_ids = lax.dynamic_slice_in_dim(group_ids.astype(jnp.int32), start, ATT_TOK, 0)
        return attend_block(query_nope, query_rope, key_block, key_ids, query_ids, w_uk, w_uv)

    attn_blocks = lax.map(one_block, (jnp.arange(N_SEQ, dtype=jnp.int32), query_blocks, rope_blocks))
    attn_out = attn_blocks.reshape(ATT_ROWS, HEADS * VDIM)

    flat_ids = expert_ids.astype(jnp.int32).reshape(N_SEQ, MOE_TOK * TOPW)
    onehot = (flat_ids[..., None] == jnp.arange(EXPERTS, dtype=jnp.int32)).astype(jnp.int32)
    before = jnp.cumsum(onehot, axis=1) - onehot
    slot_of = jnp.sum(before * onehot, axis=2).reshape(MOE_ROWS, TOPW)
    block_of = jnp.broadcast_to((jnp.arange(MOE_ROWS, dtype=jnp.int32) // MOE_TOK)[:, None], (MOE_ROWS, TOPW))
    pair_ids = jnp.arange(MOE_ROWS * TOPW, dtype=jnp.int32).reshape(MOE_ROWS, TOPW)
    table = jnp.full((EXPERTS, N_SEQ, CAP), MOE_ROWS * TOPW, jnp.int32)
    table = table.at[expert_ids.astype(jnp.int32), block_of, slot_of].set(pair_ids)
    padded_in = jnp.concatenate([moe_in, jnp.zeros((1, D), jnp.bfloat16)], axis=0)
    padded_gate = jnp.concatenate([gate_w.reshape(-1), jnp.zeros((1,), jnp.float32)])

    def one_expert(accum, inputs):
        slot_pairs, gate_mat, up_mat, down_mat = inputs
        token_idx = slot_pairs // TOPW
        chosen = padded_in[token_idx]
        gate_pre = jnp.dot(chosen, gate_mat, preferred_element_type=jnp.float32)
        up_pre = jnp.dot(chosen, up_mat, preferred_element_type=jnp.float32)
        hidden = (jax.nn.silu(gate_pre) * up_pre).astype(jnp.bfloat16)
        expert_out = jnp.dot(hidden, down_mat, preferred_element_type=jnp.float32).astype(jnp.bfloat16)
        expert_out = lax.optimization_barrier(expert_out)
        weight = padded_gate[slot_pairs]
        accum = accum.at[token_idx].add(weight[:, None] * expert_out.astype(jnp.float32))
        return accum, None

    start_acc = jnp.zeros((MOE_ROWS + 1, D), jnp.float32)
    accum, _ = lax.scan(one_expert, start_acc, (table.reshape(EXPERTS, N_SEQ * CAP), w_gate, w_up, w_down))
    moe_out = (moe_in.astype(jnp.float32) + accum[:MOE_ROWS]).astype(jnp.bfloat16)
    return attn_out, moe_out
```

```python
import functools
import jax
import jax.numpy as jnp
from jax import lax
from jax.experimental import pallas as pl
from jax.experimental.pallas import tpu as pltpu
from jax.sharding import PartitionSpec as P


def passed_along(value, axis, steps):
    count = lax.axis_size(axis)
    initial, last = (max(0, -steps), min(count, count - steps))
    return lax.ppermute(value, axis, [(source, source + steps) for source in range(initial, last)])


def attend_local(query_nope, query_rope, all_keys, key_ids, query_ids, w_uk, w_uv):
    tok_count = query_nope.shape[0]
    head_count = w_uk.shape[0]
    nope_width = w_uk.shape[1]
    lat_width = w_uk.shape[2]
    rope_width = query_rope.shape[1] // head_count
    q_split = query_nope.reshape(tok_count, head_count, nope_width)
    r_split = query_rope.reshape(tok_count, head_count, rope_width)
    q_latent = jnp.einsum("thn,hnl->htl", q_split, w_uk, preferred_element_type=jnp.float32).astype(
        jnp.bfloat16
    )
    latent = all_keys[:, :lat_width]
    rotary = all_keys[:, lat_width:]
    scale_factor = (nope_width + rope_width) ** (-0.5)
    scores = jnp.einsum("htl,kl->htk", q_latent, latent, preferred_element_type=jnp.float32)
    scores = (
        scores + jnp.einsum("thr,kr->htk", r_split, rotary, preferred_element_type=jnp.float32)
    ) * scale_factor
    key_count = all_keys.shape[0]
    query_pos = jnp.arange(tok_count, dtype=jnp.int32) + (key_count - tok_count)
    key_pos = jnp.arange(key_count, dtype=jnp.int32)
    allowed = (key_ids[None, :] == query_ids[:, None]) & (key_pos[None, :] <= query_pos[:, None])
    scores = jnp.where(allowed[None], scores, -jnp.inf)
    highest = jnp.max(scores, axis=2, keepdims=True)
    expo = jnp.exp(scores - highest)
    probs = (expo / jnp.sum(expo, axis=2, keepdims=True)).astype(jnp.bfloat16)
    mixed_latent = jnp.einsum(
        "htk,kl->htl", probs, latent, preferred_element_type=jnp.float32
    ).astype(jnp.bfloat16)
    heads_out = jnp.einsum("htl,hlv->thv", mixed_latent, w_uv, preferred_element_type=jnp.float32)
    return heads_out.astype(jnp.bfloat16).reshape(tok_count, head_count * w_uv.shape[2])


CHAIN_PARTS = 4
F32, BF16 = jnp.float32, jnp.bfloat16


def experts_kernel(sizes, x_ref, wg_hbm, wu_hbm, wd_hbm, out_ref, wg, wu, wd, xb, rows_out, rows_in, gu, gu_in,
                   hid, back_out, back_in, near, contrib, acc_in, acc_out, load_sem, x_send, x_recv, swap_send,
                   swap_recv, gu_send, gu_recv, hid_send, hid_recv, back_send, back_recv, acc_send, acc_recv):
    tokens, width, capacity, part = sizes
    s = lax.axis_index("seq")
    h = lax.axis_index("head")
    z, core = s // 2, s % 2
    mate = s + 1 - 2 * core
    edge = (z == 0) | (z == 3)
    middle = (z == 1) | (z == 2)
    inner_z = jnp.where(z == 0, 1, jnp.where(z == 3, 2, jnp.where(z == 1, 2, 1)))
    inner = inner_z * 2 + core
    outer = jnp.where(z <= 1, 0, 3) * 2 + core
    peers = [jnp.where(h % 2 == 0, h + 1, h - 1), (h + 2) % 4, 3 - h]

    loads = []
    for at, (source, target) in enumerate(((wg_hbm, wg), (wu_hbm, wu), (wd_hbm, wd))):
        copy = pltpu.make_async_copy(source, target, load_sem.at[at])
        copy.start()
        loads.append(copy)

    barrier = pltpu.get_barrier_semaphore()
    pl.semaphore_signal(barrier, inc=1, device_id={"seq": mate}, device_id_type=pl.DeviceIdType.MESH)
    pl.semaphore_signal(barrier, inc=1, device_id={"seq": inner}, device_id_type=pl.DeviceIdType.MESH)
    for peer in peers:
        pl.semaphore_signal(barrier, inc=1, device_id={"head": peer}, device_id_type=pl.DeviceIdType.MESH)

    @pl.when(middle)
    def _():
        pl.semaphore_signal(barrier, inc=1, device_id={"seq": outer}, device_id_type=pl.DeviceIdType.MESH)

    @pl.when(middle)
    def _():
        pl.semaphore_wait(barrier, 6)

    @pl.when(edge)
    def _():
        pl.semaphore_wait(barrier, 5)

    def remote(source, target, send, recv, **device):
        return pltpu.make_async_remote_copy(
            src_ref=source, dst_ref=target, send_sem=send, recv_sem=recv, device_id=device,
            device_id_type=pl.DeviceIdType.MESH,
        )

    sent = []

    def send_when(condition, copy):
        pl.when(condition)(copy.start)
        sent.append((condition, copy))

    def send(copy):
        copy.start()
        sent.append((None, copy))

    send_when((z == 0) | middle, remote(x_ref, xb.at[1], x_send.at[0], x_recv.at[1],
                                        seq=jnp.where(z == 0, inner, outer)))
    send_when(z == 1, remote(x_ref, xb.at[1], x_send.at[1], x_recv.at[1], seq=inner))
    send_when((z == 2) | (z == 3), remote(x_ref, xb.at[2], x_send.at[1], x_recv.at[2], seq=inner))

    def x_wait(slot):
        remote(x_ref, xb.at[slot], x_send.at[0], x_recv.at[slot], seq=inner).wait_recv()

    row_at = lax.broadcasted_iota(jnp.int32, (tokens, tokens), 0)
    col_at = lax.broadcasted_iota(jnp.int32, (tokens, tokens), 1)
    earlier = (row_at < col_at).astype(F32).astype(BF16)
    slots = lax.broadcasted_iota(jnp.int32, (capacity, tokens), 0).astype(F32)

    def placing(block, expert):
        info = block[tokens:tokens + 16, 0:tokens].astype(F32)
        number = expert.astype(F32)
        first = (info[0:1] == number).astype(F32)
        second = (info[1:2] == number).astype(F32)
        hit = first + second
        gate = first * (info[2:3] + info[3:4] + info[4:5]) + second * (info[5:6] + info[6:7] + info[7:8])
        hits = jnp.broadcast_to(hit, (16, tokens)).astype(BF16)
        slot = jnp.dot(hits, earlier, preferred_element_type=F32)[0:1]
        pick = jnp.where(slots == slot, 1.0, 0.0) * hit
        return pick, jnp.sum(pick * gate, axis=1, keepdims=True)

    def block_of(step):
        return x_ref if step == 0 else xb.at[step]

    def pick_rows(step):
        block = block_of(step)
        mine, _ = placing(block, s)
        theirs, _ = placing(block, mate)
        picked = jnp.dot(theirs.astype(BF16), block[0:tokens, :], preferred_element_type=F32)
        rows_out[step] = picked.astype(BF16)
        send(remote(rows_out.at[step], rows_in.at[step, 1], swap_send.at[step], swap_recv.at[step], seq=mate))
        picked = jnp.dot(mine.astype(BF16), block[0:tokens, :], preferred_element_type=F32)
        rows_in[step, 0] = picked.astype(BF16)

    def gate_up(step):
        remote(rows_out.at[step], rows_in.at[step, 1], swap_send.at[step], swap_recv.at[step], seq=mate).wait_recv()
        rows = rows_in[step].reshape(2 * capacity, width)

        @pl.loop(0, 4)
        def _(q):
            columns = pl.ds(pl.multiple_of(q * part, part), part)
            gu[step, q, :, 0:part] = jnp.dot(rows, wg[:, columns], preferred_element_type=F32).astype(BF16)
            gu[step, q, :, part:2 * part] = jnp.dot(rows, wu[:, columns], preferred_element_type=F32).astype(BF16)

        for at, peer in enumerate(peers):
            send(remote(gu.at[step, peer], gu_in.at[step, at], gu_send.at[step, at], gu_recv.at[step, at], head=peer))

    def hidden(step):
        total = gu[step, h].astype(F32)
        for at, peer in enumerate(peers):
            remote(gu.at[step, peer], gu_in.at[step, at], gu_send.at[step, at], gu_recv.at[step, at],
                   head=peer).wait_recv()
            total = total + gu_in[step, at].astype(F32)
        gate = total[:, 0:part]
        hid[step, h] = (gate / (1.0 + jnp.exp(-gate)) * total[:, part:2 * part]).astype(BF16)
        for at, peer in enumerate(peers):
            send(remote(hid.at[step, h], hid.at[step, h], hid_send.at[step, at], hid_recv.at[step, at], head=peer))

    def down(step):
        for at, peer in enumerate(peers):
            remote(hid.at[step, peer], hid.at[step, peer], hid_send.at[step, at], hid_recv.at[step, at],
                   head=peer).wait_recv()
        total = jnp.dot(hid[step, 0], wd[0:part, :], preferred_element_type=F32)
        for q in range(1, 4):
            total = total + jnp.dot(hid[step, q], wd[q * part:(q + 1) * part, :], preferred_element_type=F32)
        back_out[step] = total[capacity:].astype(BF16)
        send(remote(back_out.at[step], back_in.at[step], back_send.at[step], back_recv.at[step], seq=mate))
        near[step] = total[0:capacity].astype(BF16)

    def combine(step):
        block = block_of(step)
        mine, mine_weight = placing(block, s)
        theirs, theirs_weight = placing(block, mate)
        first = (near[step].astype(F32) * mine_weight).astype(BF16)
        value = jnp.dot(mine.T.astype(BF16), first, preferred_element_type=F32)
        remote(back_out.at[step], back_in.at[step], back_send.at[step], back_recv.at[step], seq=mate).wait_recv()
        second = (back_in[step].astype(F32) * theirs_weight).astype(BF16)
        value = value + jnp.dot(theirs.T.astype(BF16), second, preferred_element_type=F32)
        contrib[step] = value.astype(BF16)

    pieces = CHAIN_PARTS
    piece = width // pieces

    def acc_copy(source, slot, at, to):
        return remote(source, acc_in.at[slot, at], acc_send.at[slot, at], acc_recv.at[slot, at], seq=to)

    def acc_wait(slot, at):
        acc_copy(acc_out.at[0, at], slot, at, inner).wait_recv()

    def cut(ref, at):
        return ref[:, at * piece:(at + 1) * piece].astype(F32)

    pick_rows(0)
    for copy in loads[:2]:
        copy.wait()
    gate_up(0)
    hidden(0)
    loads[2].wait()
    x_wait(1)
    send_when(z == 1, remote(xb.at[1], xb.at[3], x_send.at[2], x_recv.at[3], seq=inner))
    send_when(z == 2, remote(xb.at[1], xb.at[2], x_send.at[2], x_recv.at[2], seq=outer))
    pl.when(middle)(lambda: x_wait(2))
    send_when(z == 1, remote(xb.at[2], xb.at[2], x_send.at[3], x_recv.at[2], seq=outer))
    send_when(z == 2, remote(xb.at[2], xb.at[3], x_send.at[3], x_recv.at[3], seq=inner))
    pick_rows(1)
    down(0)
    gate_up(1)
    combine(0)
    hidden(1)
    pl.when(edge)(lambda: x_wait(2))
    pl.when(middle)(lambda: x_wait(3))
    send_when(middle, remote(xb.at[3], xb.at[3], x_send.at[4], x_recv.at[3], seq=outer))
    pick_rows(2)
    down(1)
    gate_up(2)
    combine(1)

    def put_pieces(slot, step):
        for at in range(pieces):
            acc_out[slot, at] = contrib[step, :, at * piece:(at + 1) * piece]

    def from_edges(slot, step):
        pl.when(edge)(lambda: put_pieces(slot, step))
        for at in range(pieces):
            send_when(edge, acc_copy(acc_out.at[slot, at], slot, at, inner))

    from_edges(0, 1)
    hidden(2)
    pl.when(edge)(lambda: x_wait(3))
    pick_rows(3)
    down(2)
    gate_up(3)
    combine(2)
    from_edges(1, 2)
    hidden(3)

    def add_second():
        for at in range(pieces):
            acc_wait(1, at)
            here = jnp.where(z == 1, cut(contrib.at[2], at), cut(contrib.at[1], at))
            acc_out[2, at] = (here + acc_in[1, at].astype(F32)).astype(BF16)

    down(3)
    combine(3)
    from_edges(3, 3)
    pl.when(middle)(add_second)
    for at in range(pieces):
        send_when(middle, acc_copy(acc_out.at[2, at], 2, at, inner))
    for at in range(pieces):
        def add_third(at=at):
            acc_wait(3, at)
            acc_out[4, at] = (cut(contrib.at[3], at) + acc_in[3, at].astype(F32)).astype(BF16)

        pl.when(middle)(add_third)
        send_when(middle, acc_copy(acc_out.at[4, at], 4, at, inner))
    for at in range(pieces):
        def add_last(at=at):
            acc_wait(4, at)
            here = jnp.where(z == 2, cut(contrib.at[2], at), cut(contrib.at[1], at))
            acc_out[5, at] = (here + acc_in[4, at].astype(F32)).astype(BF16)

        pl.when(middle)(add_last)
        send_when(middle, acc_copy(acc_out.at[5, at], 5, at, outer))
    for at in range(pieces):
        span = slice(at * piece, (at + 1) * piece)

        def finish_middle(at=at, span=span):
            acc_wait(0, at)
            acc_wait(2, at)
            total = x_ref[0:tokens, span].astype(F32) + contrib[0, :, span].astype(F32)
            total = total + acc_in[0, at].astype(F32) + acc_in[2, at].astype(F32)
            out_ref[:, span] = total.astype(BF16)

        pl.when(middle)(finish_middle)
    for at in range(pieces):
        span = slice(at * piece, (at + 1) * piece)

        def finish_edge(at=at, span=span):
            total = x_ref[0:tokens, span].astype(F32) + contrib[0, :, span].astype(F32)
            acc_wait(5, at)
            out_ref[:, span] = (total + acc_in[5, at].astype(F32)).astype(BF16)

        pl.when(edge)(finish_edge)
    for condition, copy in sent:
        if condition is None:
            copy.wait_send()
        else:
            pl.when(condition)(copy.wait_send)


def experts_on_line(moe_in, expert_ids, gate_w, w_gate, w_up, w_down):
    tokens, width = moe_in.shape
    units = w_gate.shape[1]
    capacity, part, pieces = tokens // 2, units // 4, CHAIN_PARTS
    high = lax.reduce_precision(gate_w, 8, 7)
    mid = lax.reduce_precision(gate_w - high, 8, 7)
    low = gate_w - high - mid
    info = jnp.stack(
        [expert_ids[:, 0].astype(F32), expert_ids[:, 1].astype(F32)]
        + [v[:, k] for k in (0, 1) for v in (high, mid, low)]
    )
    info = jnp.pad(info, ((0, 8), (0, width - tokens))).astype(BF16)
    block = jnp.concatenate([moe_in, info], axis=0)
    vmem, dma = pltpu.VMEM, pltpu.SemaphoreType.DMA
    flops = 2 * 8 * capacity * width * units * 3
    return pl.pallas_call(
        functools.partial(experts_kernel, (tokens, width, capacity, part)),
        out_shape=jax.ShapeDtypeStruct((tokens, width), BF16),
        in_specs=[pl.BlockSpec(memory_space=pltpu.VMEM)] + [pl.BlockSpec(memory_space=pl.ANY)] * 3,
        out_specs=pl.BlockSpec(memory_space=pltpu.VMEM),
        scratch_shapes=[
            vmem((width, units), BF16),
            vmem((width, units), BF16),
            vmem((units, width), BF16),
            vmem((4, tokens + 16, width), BF16),
            vmem((4, capacity, width), BF16),
            vmem((4, 2, capacity, width), BF16),
            vmem((4, 4, 2 * capacity, 2 * part), BF16),
            vmem((4, 3, 2 * capacity, 2 * part), BF16),
            vmem((4, 4, 2 * capacity, part), BF16),
            vmem((4, capacity, width), BF16),
            vmem((4, capacity, width), BF16),
            vmem((4, capacity, width), BF16),
            vmem((4, tokens, width), BF16),
            vmem((6, pieces, tokens, width // pieces), BF16),
            vmem((6, pieces, tokens, width // pieces), BF16),
            dma((3,)),
            dma((5,)),
            dma((4,)),
            dma((4,)),
            dma((4,)),
            dma((4, 3)),
            dma((4, 3)),
            dma((4, 3)),
            dma((4, 3)),
            dma((4,)),
            dma((4,)),
            dma((6, pieces)),
            dma((6, pieces)),
        ],
        compiler_params=pltpu.CompilerParams(
            collective_id=0, has_side_effects=True, vmem_limit_bytes=60 * 1024 * 1024
        ),
        cost_estimate=pl.CostEstimate(flops=flops, bytes_accessed=16 * 1024 * 1024, transcendentals=0),
    )(block, w_gate, w_up, w_down)


def on_device(
    q_nope,
    q_rope,
    kv_latent,
    group_ids,
    w_uk,
    w_uv,
    moe_in,
    expert_ids,
    gate_w,
    w_gate,
    w_up,
    w_down,
):
    att_rows = kv_latent.shape[0]
    earlier = passed_along(kv_latent, "seq", 1)
    all_keys = jnp.concatenate([earlier, kv_latent], axis=0)
    padded_ids = jnp.concatenate([jnp.full((att_rows,), -1, jnp.int32), group_ids])
    row_start = lax.axis_index("seq") * att_rows
    key_ids = lax.dynamic_slice_in_dim(padded_ids, row_start, 2 * att_rows, 0)
    query_ids = lax.dynamic_slice_in_dim(group_ids, row_start, att_rows, 0)
    tokens_here = moe_in.shape[0]
    feat_width = moe_in.shape[1]
    top_count = expert_ids.shape[1]
    if (lax.axis_size("seq"), lax.axis_size("head"), top_count) == (8, 4, 2):
        attn_out = attend_local(q_nope, q_rope, all_keys, key_ids, query_ids, w_uk, w_uv)
        moe_out = experts_on_line(moe_in, expert_ids, gate_w, w_gate[0], w_up[0], w_down[0])
        return (attn_out, moe_out)
    expert_count = lax.axis_size("seq")
    capacity = 2 * tokens_here * top_count // expert_count
    flat_ids = expert_ids.reshape(-1)
    onehot = (flat_ids[:, None] == jnp.arange(expert_count, dtype=jnp.int32)[None, :]).astype(
        jnp.int32
    )
    order = jnp.arange(flat_ids.shape[0], dtype=jnp.int32)
    before = jnp.dot(
        (order[None, :] < order[:, None]).astype(jnp.bfloat16),
        onehot.astype(jnp.bfloat16),
        preferred_element_type=jnp.float32,
    ).astype(jnp.int32)
    slot_of = jnp.sum(before * onehot, axis=1)
    target = flat_ids * capacity + slot_of
    placing = (
        jnp.arange(expert_count * capacity, dtype=jnp.int32)[:, None] == target[None, :]
    ).astype(jnp.bfloat16)
    to_token = jnp.sum(placing.reshape(expert_count * capacity, tokens_here, top_count), axis=2)
    outgoing = jnp.dot(to_token, moe_in, preferred_element_type=jnp.float32).astype(jnp.bfloat16)
    outgoing = outgoing.reshape(expert_count, capacity, feat_width)
    gate_local = w_gate[0]
    up_local = w_up[0]
    down_local = w_down[0]
    arrived = lax.all_to_all(outgoing, "seq", split_axis=0, concat_axis=0, tiled=True)
    sources, items, width = arrived.shape
    row_block = arrived.reshape(sources * items, width)
    gate_part = jnp.dot(row_block, gate_local, preferred_element_type=jnp.float32)
    up_part = jnp.dot(row_block, up_local, preferred_element_type=jnp.float32)
    gate_sum = lax.psum_scatter(gate_part, "head", scatter_dimension=1, tiled=True)
    up_sum = lax.psum_scatter(up_part, "head", scatter_dimension=1, tiled=True)
    hidden_part = (jax.nn.silu(gate_sum) * up_sum).astype(jnp.bfloat16)
    hidden = lax.all_gather(hidden_part, "head", axis=1, tiled=True)
    result = jnp.dot(hidden, down_local, preferred_element_type=jnp.float32).astype(jnp.bfloat16)
    processed = result.reshape(sources, items, width)
    attn_out = attend_local(q_nope, q_rope, all_keys, key_ids, query_ids, w_uk, w_uv)
    returned = lax.all_to_all(processed, "seq", split_axis=0, concat_axis=0, tiled=True)
    picked = jnp.einsum(
        "pr,pw->rw",
        placing,
        returned.reshape(expert_count * capacity, feat_width),
        preferred_element_type=jnp.float32,
    )
    picked = picked.reshape(tokens_here, top_count, feat_width)
    mixed = jnp.sum(gate_w[:, :, None] * picked, axis=1)
    moe_out = (moe_in.astype(jnp.float32) + mixed).astype(jnp.bfloat16)
    return (attn_out, moe_out)


def solution(mesh):
    return jax.shard_map(
        on_device,
        mesh=mesh,
        in_specs=(
            P("seq", "head"),
            P("seq", "head"),
            P("seq", None),
            P(),
            P("head", None, None),
            P("head", None, None),
            P("seq", "head"),
            P("seq", None),
            P("seq", None),
            P("seq", "head", None),
            P("seq", "head", None),
            P("seq", None, "head"),
        ),
        out_specs=(P("seq", "head"), P("seq", "head")),
        check_vma=False,
    )
```
